32 devices in a mesh: dp: 4 (over y, x), blk: 8 (over z, core).
Axes of the slice: x: 2, y: 2, z: 4, core: 2. Of those that a mesh axis runs over, the one named last changes fastest.
Arguments:
- inputs: bfloat16 [4, 2048, 1024], P('dp', 'blk'), may hold values from -6 to 6
- upstream: bfloat16 [4, 2048, 1024], P('dp', 'blk'), may hold values from -6 to 6
- gain: float32 [1024], replicated, may hold values from 0.5 to 1.5
- w_query: bfloat16 [1024, 1024], replicated
- w_key: bfloat16 [1024, 256], replicated
- w_value: bfloat16 [1024, 256], replicated, may hold values from -0.1875 to 0.1875
- w_out: bfloat16 [1024, 1024], replicated, may hold values from -0.1875 to 0.1875
- prefix_len: int32 [4], P('dp'), may hold values from 256 to 1984
- bound: int32 [4], P('dp'), may hold values from 0 to 15
Outputs:
- d_inputs: bfloat16 [4, 2048, 1024], P('dp', 'blk')
- d_query: float32 [1024, 1024], P('blk')
- d_key: float32 [1024, 256], P('blk')
- d_value: float32 [1024, 256], P('blk')
- d_out: float32 [1024, 1024], P('blk')
- d_gain: float32 [1024], P('blk')
The draws below stay inside these ranges and needn't reach their ends.
All inputs are finite; a program needn't handle non-finite values.
Results may differ from the reference program's by a relative error of at most 0.02.
The reference program's roundings to bfloat16 on the way (of `hidden`, `query`, `d_attn`, `probs_b`, `attn`, `dscores`, `dq` and `dk`) count: a program that leaves them out, or rounds other values in their place, can miss the bound.
Values may be sent and summed in bfloat16 or wider, within the bound.
A program may use at most 128 MiB of HBM per device.

```python
import jax
import jax.numpy as jnp
from jax import lax

D = 1024
HEADS = 4
HS = 256
ACT = 64
BLOCK = 128
HQ = 1024
SEQ = 2048
EPISODES = 4


def paired_weights(key):
    base_query = jax.random.normal(jax.random.fold_in(key, 11), (D, HEADS * HS), jnp.float32) * D ** (-0.5)
    base_key = jax.random.normal(jax.random.fold_in(key, 12), (D, HS), jnp.float32) * D ** (-0.5)
    return (base_query, base_key)


def draw_w_query(key, part):
    return paired_weights(key)[0].astype(jnp.bfloat16)


def draw_w_key(key, part):
    return paired_weights(key)[1].astype(jnp.bfloat16)


def touch_ends(entries, own_key, low, top_value):
    index_at = [jax.random.randint(jax.random.fold_in(own_key, axis), (), 0, length) for axis, length in enumerate(entries.shape)]
    longest = entries.shape.index(max(entries.shape))
    next_to = index_at[:longest] + [(index_at[longest] + 1) % entries.shape[longest]] + index_at[longest + 1:]
    return entries.at[tuple(index_at)].set(low).at[tuple(next_to)].set(top_value)


def shard_levels(rng, dims, shards, least, top_value):
    def one(axis_at, shards_of):
        draws = jax.random.uniform(jax.random.fold_in(jax.random.fold_in(rng, 6), axis_at), (shards_of,), jnp.float32, least / len(shards), top_value / len(shards))
        return jnp.repeat(jnp.exp(draws), dims[axis_at] // shards_of).reshape((-1,) + (1,) * (len(dims) - axis_at - 1))

    level = one(*shards[0])
    for cut in shards[1:]:
        level = level * one(*cut)
    return level


def noise(stream_key, shape, width, most, shards=(), kind=jnp.bfloat16):
    values = jax.random.normal(stream_key, shape, jnp.float32) * width
    if len(shards) > 0:
        values = shard_levels(stream_key, shape, shards, -0.22, 0.18) * values
    return jnp.clip(values, min=-most, max=most).astype(kind)


def setup_inputs(seed: int = 0) -> dict:
    splits = jax.random.split(jax.random.key(seed), 10)
    return {
        "inputs": noise(splits[0], (EPISODES, SEQ, D), 1.0, 6.0, ((0, 4), (1, 8))),
        "upstream": noise(splits[1], (EPISODES, SEQ, D), 1.0, 6.0, ((0, 4), (1, 8))),
        "gain": jnp.clip(1.0 + 0.1 * jax.random.normal(splits[2], (D,), jnp.float32), 0.5, 1.5),
        "w_query": draw_w_query(jax.random.fold_in(splits[9], 71), 0),
        "w_key": draw_w_key(jax.random.fold_in(splits[9], 71), 0),
        "w_value": noise(splits[5], (D, HS), D ** -0.5, 0.1875),
        "w_out": noise(splits[6], (HQ, D), HQ ** -0.5, 0.1875),
        "prefix_len": touch_ends(jax.random.randint(splits[7], (EPISODES,), SEQ // 8, SEQ - ACT + 1), jax.random.fold_in(splits[7], 1), SEQ // 8, SEQ - ACT).astype(jnp.int32),
        "bound": touch_ends(jax.random.randint(splits[8], (EPISODES,), 0, SEQ // BLOCK), jax.random.fold_in(splits[8], 1), 0, (SEQ // BLOCK) - 1).astype(jnp.int32),
    }


EPS = 1e-06
NEG = -1e+30

def episode_grads(inputs, upstream, plen, edge_block, gain, w_query, w_key, w_value, w_out):
    scaling = HS ** (-0.5)
    xf = inputs.astype(jnp.float32)
    inv = lax.rsqrt(lax.optimization_barrier(jnp.mean(xf * xf, axis=-1, keepdims=True)) + EPS)
    normed = xf * inv
    hidden = (normed * gain).astype(jnp.bfloat16)
    query = jnp.dot(hidden, w_query, preferred_element_type=jnp.float32).astype(jnp.bfloat16)
    keys = jnp.dot(hidden, w_key, preferred_element_type=jnp.float32).astype(jnp.bfloat16)
    values = jnp.dot(hidden, w_value, preferred_element_type=jnp.float32).astype(jnp.bfloat16)
    d_attn = jnp.dot(upstream, w_out.T, preferred_element_type=jnp.float32).astype(jnp.bfloat16)
    pos = jnp.arange(SEQ, dtype=jnp.int32)
    key_ok = (pos < plen) | (pos >= SEQ - ACT)
    visible = key_ok[None, :] & ((pos[None, :] < BLOCK * edge_block) | (pos[None, :] <= pos[:, None]))
    q_heads = query.reshape(SEQ, HEADS, HS).transpose(1, 0, 2)
    a_heads = d_attn.reshape(SEQ, HEADS, HS).transpose(1, 0, 2)

    def one_head(pair):
        q_one, da_one = pair
        scores = jnp.dot(q_one, keys.T, preferred_element_type=jnp.float32) * scaling
        scores = jnp.where(visible, scores, NEG)
        top = lax.optimization_barrier(jnp.max(scores, axis=-1, keepdims=True))
        expo = jnp.exp(scores - top)
        probs = expo / lax.optimization_barrier(jnp.sum(expo, axis=-1, keepdims=True))
        probs_b = probs.astype(jnp.bfloat16)
        attn = jnp.dot(probs_b, values, preferred_element_type=jnp.float32).astype(jnp.bfloat16)
        dprobs = jnp.dot(da_one, values.T, preferred_element_type=jnp.float32)
        delta = lax.optimization_barrier(jnp.sum(da_one.astype(jnp.float32) * attn.astype(jnp.float32), axis=-1, keepdims=True))
        dscores = (probs * (dprobs - delta)).astype(jnp.bfloat16)
        dq = jnp.dot(dscores, keys, preferred_element_type=jnp.float32) * scaling
        dk = jnp.dot(dscores.T, q_one, preferred_element_type=jnp.float32) * scaling
        dv = jnp.dot(probs_b.T, da_one, preferred_element_type=jnp.float32)
        return (attn, dq, dk, dv)
    attn_h, dq_h, dk_h, dv_h = lax.map(one_head, (q_heads, a_heads))
    attn = attn_h.transpose(1, 0, 2).reshape(SEQ, HEADS * HS)
    dq = dq_h.transpose(1, 0, 2).reshape(SEQ, HEADS * HS).astype(jnp.bfloat16)
    dk = lax.optimization_barrier(jnp.sum(dk_h, axis=0)).astype(jnp.bfloat16)
    dv = lax.optimization_barrier(jnp.sum(dv_h, axis=0)).astype(jnp.bfloat16)
    dhidden = jnp.dot(dq, w_query.T, preferred_element_type=jnp.float32)
    dhidden = dhidden + jnp.dot(dk, w_key.T, preferred_element_type=jnp.float32)
    dhidden = dhidden + jnp.dot(dv, w_value.T, preferred_element_type=jnp.float32)
    g_query = jnp.dot(hidden.T, dq, preferred_element_type=jnp.float32)
    g_key = jnp.dot(hidden.T, dk, preferred_element_type=jnp.float32)
    g_value = jnp.dot(hidden.T, dv, preferred_element_type=jnp.float32)
    g_out = jnp.dot(attn.T, upstream, preferred_element_type=jnp.float32)
    g_gain = lax.optimization_barrier(jnp.sum(dhidden * normed, axis=0))
    scaled = dhidden * gain
    d_in = upstream.astype(jnp.float32) + inv * (scaled - normed * lax.optimization_barrier(jnp.mean(scaled * normed, axis=-1, keepdims=True)))
    return (d_in.astype(jnp.bfloat16), g_query, g_key, g_value, g_out, g_gain)

def reference(inputs, upstream, gain, w_query, w_key, w_value, w_out, prefix_len, bound):

    def per_episode(item):
        x_one, g_one, plen, edge_block = item
        return episode_grads(x_one, g_one, plen, edge_block, gain, w_query, w_key, w_value, w_out)
    d_in, g_query, g_key, g_value, g_out, g_gain = lax.map(per_episode, (inputs, upstream, prefix_len, bound))
    return (d_in, lax.optimization_barrier(jnp.sum(g_query, axis=0)), lax.optimization_barrier(jnp.sum(g_key, axis=0)), lax.optimization_barrier(jnp.sum(g_value, axis=0)), lax.optimization_barrier(jnp.sum(g_out, axis=0)), lax.optimization_barrier(jnp.sum(g_gain, axis=0)))
```

```python
import functools

import jax
import jax.numpy as jnp
from jax import lax
from jax.experimental import pallas as pl
from jax.experimental.pallas import tpu as pltpu
from jax.sharding import PartitionSpec as P

HS = 256
ACT = 64
BLOCK = 128
EPS = 1e-06
NEG = -1e30
CHUNK = 256
F32 = jnp.float32
BF16 = jnp.bfloat16
MESH = pl.DeviceIdType.MESH


def dot_nn(left, right):
    return lax.dot_general(left, right, (((1,), (0,)), ((), ())), preferred_element_type=F32)


def dot_nt(left, right):
    return lax.dot_general(left, right, (((1,), (1,)), ((), ())), preferred_element_type=F32)


def dot_tn(left, right):
    return lax.dot_general(left, right, (((0,), (0,)), ((), ())), preferred_element_type=F32)


class Sizes:
    def __init__(self, n_dp, n_blk, tok, width, hq):
        self.n_dp = n_dp
        self.n_blk = n_blk
        self.chips = n_blk // 2
        self.tok = tok
        self.width = width
        self.heads = hq // HS
        self.lanes = self.heads * tok
        self.rows = width // n_blk
        self.row_parts = min(n_dp, self.rows // 16)
        self.col_parts = n_dp // self.row_parts
        self.part_rows = self.rows // self.row_parts

    def item_scratch(self, cols):
        part = (self.part_rows, cols // self.col_parts)
        vm, dma = pltpu.VMEM, pltpu.SemaphoreType.DMA
        return [
            vm((self.chips, self.rows, cols), BF16),
            vm((self.chips, self.rows, cols), BF16),
            vm((self.n_dp, self.chips, *part), BF16),
            vm((self.n_dp - 1, self.chips, *part), BF16),
            vm((self.chips, *part), BF16),
            vm((self.chips - 1, *part), BF16),
            vm((self.n_dp, *part), BF16),
            dma((2,)),
            dma((2, self.n_dp)),
            dma((2, self.chips)),
            dma((2, self.n_dp)),
        ]


class Place:
    def __init__(self, sz):
        self.dp = lax.axis_index("dp")
        self.blk = lax.axis_index("blk")
        self.core = lax.rem(self.blk, 2)
        self.chip = self.blk // 2
        self.sz = sz

    def sibling(self):
        return (self.dp, 2 * self.chip + 1 - self.core)

    def chip_at(self, offset):
        return lax.rem(self.chip + offset + self.sz.chips, self.sz.chips)

    def on_chip(self, chip):
        return (self.dp, 2 * chip + self.core)

    def dp_at(self, offset):
        return lax.rem(self.dp + offset + self.sz.n_dp, self.sz.n_dp)

    def on_dp(self, dp):
        return (dp, self.blk)


def send(src, dst, sems, index, device):
    copy = pltpu.make_async_remote_copy(
        src_ref=src, dst_ref=dst, send_sem=sems.at[(0, *index)], recv_sem=sems.at[(1, *index)],
        device_id=device, device_id_type=MESH,
    )
    return copy


class Item:
    def __init__(self, place, cols, refs):
        self.at = place
        self.sz = place.sz
        self.cols = cols
        (self.pair_out, self.pair_in, self.dp_out, self.dp_in, self.z_out, self.z_in, self.final,
         self.pair_sem, self.dp_sem, self.z_sem, self.all_sem) = refs

    def product(self, lhs_ref, rhs_ref, core, first):
        sz = self.sz
        left = jnp.concatenate([lhs_ref[2 * z + core] for z in range(sz.chips)], axis=0)
        out = dot_nn(left, rhs_ref[:, first:first + CHUNK])
        return out.reshape(sz.chips, sz.rows, CHUNK)

    def pair_copy(self):
        return send(self.pair_out, self.pair_in, self.pair_sem, (), self.at.sibling())

    def dp_copy(self, e):
        peer = self.at.dp_at(e)
        return send(self.dp_out.at[peer], self.dp_in.at[e - 1], self.dp_sem, (e,), self.at.on_dp(peer))

    def z_copy(self, d):
        chip = self.at.chip_at(d)
        return send(self.z_out.at[chip], self.z_in.at[d - 1], self.z_sem, (d,), self.at.on_chip(chip))

    def all_copy(self, e):
        mine = self.final.at[self.at.dp]
        return send(mine, mine, self.all_sem, (e,), self.at.on_dp(self.at.dp_at(e)))

    def all_arrival(self, e):
        slot = self.final.at[self.at.dp_at(-e)]
        return send(slot, slot, self.all_sem, (e,), self.at.on_dp(self.at.dp_at(e)))

    def start(self, lhs_ref, rhs_ref):
        for first in range(0, self.cols, CHUNK):
            out = self.product(lhs_ref, rhs_ref, 1 - self.at.core, first)
            self.pair_out[:, :, first:first + CHUNK] = out.astype(BF16)
        self.pair_copy().start()

    def over_dp(self, lhs_ref, rhs_ref):
        sz = self.sz
        self.pair_copy().wait_recv()
        part_cols = self.cols // sz.col_parts
        for first in range(0, self.cols, CHUNK):
            out = self.product(lhs_ref, rhs_ref, self.at.core, first)
            out = (out + self.pair_in[:, :, first:first + CHUNK].astype(F32)).astype(BF16)
            col = first // part_cols
            inner = first - col * part_cols
            for row in range(sz.row_parts):
                self.dp_out[row * sz.col_parts + col, :, :, inner:inner + CHUNK] = out[
                    :, row * sz.part_rows:(row + 1) * sz.part_rows, :
                ]
        for e in range(1, sz.n_dp):
            self.dp_copy(e).start()

    def over_chips(self):
        sz = self.sz
        total = self.dp_out[self.at.dp].astype(F32)
        for e in range(1, sz.n_dp):
            self.dp_copy(e).wait_recv()
            total = total + self.dp_in[e - 1].astype(F32)
        self.z_out[...] = total.astype(BF16)
        for d in range(1, sz.chips):
            self.z_copy(d).start()

    def to_all(self):
        sz = self.sz
        total = self.z_out[self.at.chip].astype(F32)
        for d in range(1, sz.chips):
            self.z_copy(d).wait_recv()
            total = total + self.z_in[d - 1].astype(F32)
        self.final[self.at.dp] = total.astype(BF16)
        for e in range(1, sz.n_dp):
            self.all_copy(e).start()

    def finish(self, outs):
        sz = self.sz
        for e in range(1, sz.n_dp):
            self.all_arrival(e).wait_recv()
        part_cols = self.cols // sz.col_parts
        out_cols = outs[0].shape[1]
        for part in range(sz.n_dp):
            row, col = part // sz.col_parts, part % sz.col_parts
            for first in range(0, part_cols, CHUNK):
                at = col * part_cols + first
                outs[at // out_cols][
                    row * sz.part_rows:(row + 1) * sz.part_rows,
                    at % out_cols:at % out_cols + CHUNK,
                ] = self.final[part, :, first:first + CHUNK].astype(F32)
        self.pair_copy().wait_send()
        for e in range(1, sz.n_dp):
            self.dp_copy(e).wait_send()
            self.all_copy(e).wait_send()
        for d in range(1, sz.chips):
            self.z_copy(d).wait_send()


def kernel(
    sz, plen_ref, bound_ref, x_ref, up_ref, gain_ref, wq_ref, wk_ref, wv_ref, wo_ref,
    din_ref, gq_ref, gk_ref, gv_ref, go_ref, gg_ref,
    hidden, hidden_t, q_t, q_s, da_t, da_s, kv, expo, tops, sums, attn_t, delta, acc, dq, dkv,
    dhid, dkv_out, dkv_in, dkz_out, dkz_in, gain_in, gain_all,
    kv_sem, fwd_sem, dpair_sem, dz_sem, gain_sem, gain_all_sem, *item_refs,
):
    at = Place(sz)
    tok, heads, chips, lanes = sz.tok, sz.heads, sz.chips, sz.lanes
    per = len(item_refs) // 3
    hq = heads * HS
    item_out = Item(at, up_ref.shape[1], item_refs[:per])
    item_q = Item(at, hq, item_refs[per:2 * per])
    item_kv = Item(at, 2 * HS, item_refs[2 * per:])
    scaling = HS ** (-0.5)
    seq = tok * sz.n_blk

    barrier = pltpu.get_barrier_semaphore()
    for b in range(1, sz.n_blk):
        peer = (at.dp, lax.rem(at.blk + b, sz.n_blk))
        pl.semaphore_signal(barrier, inc=1, device_id=peer, device_id_type=MESH)
    for e in range(1, sz.n_dp):
        pl.semaphore_signal(barrier, inc=1, device_id=at.on_dp(at.dp_at(e)), device_id_type=MESH)

    def normed_inv():
        xf = x_ref[...].astype(F32)
        inv = lax.rsqrt(jnp.mean(xf * xf, axis=-1, keepdims=True) + EPS)
        return xf * inv, inv

    normed, _ = normed_inv()
    hidden[...] = (normed * gain_ref[...]).astype(BF16)
    kv[at.blk, :, :HS] = dot_nn(hidden[...], wk_ref[...]).astype(BF16)
    kv[at.blk, :, HS:] = dot_nn(hidden[...], wv_ref[...]).astype(BF16)
    pl.semaphore_wait(barrier, sz.n_blk - 1 + sz.n_dp - 1)

    def kv_copy(d):
        mine = kv.at[at.blk]
        return send(mine, mine, kv_sem, (d,), at.on_chip(at.chip_at(d)))

    def kv_arrival(d):
        slot = kv.at[2 * at.chip_at(-d) + at.core]
        return send(slot, slot, kv_sem, (d,), at.on_chip(at.chip_at(d)))

    def kv_forward(d):
        slot = kv.at[2 * at.chip_at(-d) + at.core]
        return send(slot, slot, fwd_sem, (d,), at.sibling())

    def kv_forwarded(d):
        slot = kv.at[2 * at.chip_at(-d) + 1 - at.core]
        return send(slot, slot, fwd_sem, (d,), at.sibling())

    for d in range(1, chips):
        kv_copy(d).start()
    kv_forward(0).start()

    for h in range(heads):
        cols = slice(h * HS, (h + 1) * HS)
        toks = slice(h * tok, (h + 1) * tok)
        one = dot_nn(hidden[...], wq_ref[:, cols])
        q_s[toks, :] = one.astype(BF16)
        q_t[:, toks] = one.T.astype(BF16)
        one = dot_nt(up_ref[...], wo_ref[cols, :])
        da_s[toks, :] = one.astype(BF16)
        da_t[:, toks] = one.T.astype(BF16)
    for b in range(sz.n_blk):
        piece = hidden[:, b * sz.rows:(b + 1) * sz.rows].astype(F32)
        hidden_t[b] = piece.T.astype(BF16)

    plen = plen_ref[0]
    edge = bound_ref[0] * BLOCK
    q_pos = at.blk * tok + lax.rem(lax.broadcasted_iota(jnp.int32, (1, lanes), 1), tok)

    def score_block(b):
        k_pos = b * tok + lax.broadcasted_iota(jnp.int32, (tok, 1), 0)
        key_ok = (k_pos < plen) | (k_pos >= seq - ACT)
        first_seen = jnp.where(key_ok, jnp.where(k_pos < edge, -1, k_pos), seq)
        for h in range(heads):
            toks = slice(h * tok, (h + 1) * tok)
            scores = dot_nn(kv[b, :, :HS], q_t[:, toks]) * scaling
            scores = jnp.where(q_pos[:, toks] >= first_seen, scores, NEG)
            top = jnp.max(scores, axis=0, keepdims=True)
            values = jnp.exp(scores - top)
            expo[b, :, toks] = values
            tops[b, :, toks] = top
            sums[b, :, toks] = jnp.sum(values, axis=0, keepdims=True)

    score_block(at.blk)

    def arrive(d, carry):
        kv_arrival(d).wait_recv()
        kv_forward(d).start()
        score_block(2 * at.chip_at(-d) + at.core)
        kv_forwarded(d - 1).wait_recv()
        score_block(2 * at.chip_at(1 - d) + 1 - at.core)
        return carry

    lax.fori_loop(1, chips, arrive, 0)
    kv_forwarded(chips - 1).wait_recv()
    score_block(2 * at.chip_at(1 - chips) + 1 - at.core)

    top = jnp.max(tops[...], axis=0)
    scale_all = jnp.exp(tops[...] - top[None])
    total = jnp.sum(scale_all * sums[...], axis=0)
    tops[...] = scale_all / total[None]

    acc[...] = jnp.zeros_like(acc)

    def attn_step(b, carry):
        for h in range(heads):
            toks = slice(h * tok, (h + 1) * tok)
            probs = expo[b, :, toks] * tops[b, :, toks]
            expo[b, :, toks] = probs
            acc[:, toks] += dot_tn(kv[b, :, HS:], probs.astype(BF16))
        return carry

    lax.fori_loop(0, sz.n_blk, attn_step, 0)

    per_head = HS // sz.rows
    for h in range(heads):
        toks = slice(h * tok, (h + 1) * tok)
        one = acc[:, toks].astype(BF16)
        delta[:, toks] = jnp.sum(da_t[:, toks].astype(F32) * one.astype(F32), axis=0, keepdims=True)
        for j in range(per_head):
            attn_t[h * per_head + j] = one[j * sz.rows:(j + 1) * sz.rows, :]

    item_out.start(attn_t, up_ref)

    acc[...] = jnp.zeros_like(acc)

    def grads_block(b):
        dk = jnp.zeros((tok, HS), F32)
        dv = jnp.zeros((tok, HS), F32)
        for h in range(heads):
            toks = slice(h * tok, (h + 1) * tok)
            probs = expo[b, :, toks]
            dprobs = dot_nn(kv[b, :, HS:], da_t[:, toks])
            dscores = (probs * (dprobs - delta[:, toks])).astype(BF16)
            acc[:, toks] += dot_tn(kv[b, :, :HS], dscores)
            dk = dk + dot_nn(dscores, q_s[toks, :])
            dv = dv + dot_nn(probs.astype(BF16), da_s[toks, :])
        return dk * scaling, dv

    def dpair_copy(d):
        chip = at.chip_at(d)
        return send(dkv_out.at[chip], dkv_in.at[chip], dpair_sem, (d,), at.sibling())

    def dz_copy(d):
        chip = at.chip_at(d)
        return send(dkz_out.at[d - 1], dkz_in.at[d - 1], dz_sem, (d,), at.on_chip(chip))

    def pair_sum(d):
        chip = at.chip_at(d)
        dk, dv = grads_block(2 * chip + 1 - at.core)
        dkv_out[chip, :, :HS] = dk.astype(BF16)
        dkv_out[chip, :, HS:] = dv.astype(BF16)
        dpair_copy(d).start()
        dk, dv = grads_block(2 * chip + at.core)
        dpair_copy(d).wait_recv()
        dk = dk + dkv_in[chip, :, :HS].astype(F32)
        dv = dv + dkv_in[chip, :, HS:].astype(F32)
        return dk, dv

    def grads_step(d, carry):
        dk, dv = pair_sum(d)
        dkz_out[d - 1, :, :HS] = dk.astype(BF16)
        dkz_out[d - 1, :, HS:] = dv.astype(BF16)
        dz_copy(d).start()
        return carry

    lax.fori_loop(1, chips, grads_step, 0)
    dk, dv = pair_sum(0)
    dhid[:, :HS] = dk
    dhid[:, HS:2 * HS] = dv

    item_out.over_dp(attn_t, up_ref)
    for h in range(heads):
        toks = slice(h * tok, (h + 1) * tok)
        dq[:, h * HS:(h + 1) * HS] = (acc[:, toks] * scaling).T.astype(BF16)
    item_q.start(hidden_t, dq)
    item_q.over_dp(hidden_t, dq)

    dk = dhid[:, :HS]
    dv = dhid[:, HS:2 * HS]
    for d in range(1, chips):
        dz_copy(d).wait_recv()
        dk = dk + dkz_in[d - 1, :, :HS].astype(F32)
        dv = dv + dkz_in[d - 1, :, HS:].astype(F32)
    dkv[:, :HS] = dk.astype(BF16)
    dkv[:, HS:] = dv.astype(BF16)
    item_kv.start(hidden_t, dkv)
    item_out.over_chips()
    for first in range(0, sz.width, CHUNK):
        cols = slice(first, first + CHUNK)
        dhid[:, cols] = (
            dot_nt(dq[...], wq_ref[cols, :])
            + dot_nt(dkv[:, :HS], wk_ref[cols, :])
            + dot_nt(dkv[:, HS:], wv_ref[cols, :])
        )
    item_kv.over_dp(hidden_t, dkv)

    def gain_copy(b):
        peer = (at.dp, lax.rem(at.blk + b, sz.n_blk))
        return send(gain_in.at[0], gain_in.at[b], gain_sem, (b,), peer)

    def gain_share(e):
        mine = gain_all.at[at.dp]
        return send(mine, mine, gain_all_sem, (e,), at.on_dp(at.dp_at(e)))

    def gain_arrival(e):
        slot = gain_all.at[at.dp_at(-e)]
        return send(slot, slot, gain_all_sem, (e,), at.on_dp(at.dp_at(e)))

    normed, inv = normed_inv()
    gain_in[0] = jnp.sum(dhid[...] * normed, axis=0, keepdims=True)
    for b in range(1, sz.n_blk):
        gain_copy(b).start()
    item_q.over_chips()
    item_out.to_all()

    normed, inv = normed_inv()
    scaled = dhid[...] * gain_ref[...]
    middle = jnp.mean(scaled * normed, axis=-1, keepdims=True)
    din_ref[...] = (up_ref[...].astype(F32) + inv * (scaled - normed * middle)).astype(BF16)

    total = gain_in[0]
    for b in range(1, sz.n_blk):
        gain_copy(b).wait_recv()
        total = total + gain_in[b]
    gain_all[at.dp] = total
    for e in range(1, sz.n_dp):
        gain_share(e).start()
    item_kv.over_chips()
    item_q.to_all()
    item_kv.to_all()
    item_out.finish((go_ref,))
    for e in range(1, sz.n_dp):
        gain_arrival(e).wait_recv()
    total = gain_all[0]
    for e in range(1, sz.n_dp):
        total = total + gain_all[e]
    for b in range(sz.n_blk):
        @pl.when(at.blk == b)
        def _():
            gg_ref[...] = total[:, b * sz.rows:(b + 1) * sz.rows]
    item_q.finish((gq_ref,))
    item_kv.finish((gk_ref, gv_ref))

    for d in range(1, chips):
        kv_copy(d).wait_send()
        dz_copy(d).wait_send()
    for d in range(chips):
        kv_forward(d).wait_send()
        dpair_copy(d).wait_send()
    for b in range(1, sz.n_blk):
        gain_copy(b).wait_send()
    for e in range(1, sz.n_dp):
        gain_share(e).wait_send()


def per_device(n_dp, n_blk, inputs, upstream, gain, w_query, w_key, w_value, w_out, prefix_len, bound):
    tok, width = inputs.shape[1:]
    hq = w_query.shape[1]
    sz = Sizes(n_dp, n_blk, tok, width, hq)
    chips = sz.chips
    vm, dma = pltpu.VMEM, pltpu.SemaphoreType.DMA
    scratch = [
        vm((tok, width), BF16),
        vm((n_blk, sz.rows, tok), BF16),
        vm((HS, sz.lanes), BF16),
        vm((sz.lanes, HS), BF16),
        vm((HS, sz.lanes), BF16),
        vm((sz.lanes, HS), BF16),
        vm((n_blk, tok, 2 * HS), BF16),
        vm((n_blk, tok, sz.lanes), F32),
        vm((n_blk, 1, sz.lanes), F32),
        vm((n_blk, 1, sz.lanes), F32),
        vm((n_blk, sz.rows, tok), BF16),
        vm((1, sz.lanes), F32),
        vm((HS, sz.lanes), F32),
        vm((tok, hq), BF16),
        vm((tok, 2 * HS), BF16),
        vm((tok, width), F32),
        vm((chips, tok, 2 * HS), BF16),
        vm((chips, tok, 2 * HS), BF16),
        vm((chips - 1, tok, 2 * HS), BF16),
        vm((chips - 1, tok, 2 * HS), BF16),
        vm((n_blk, 1, width), F32),
        vm((n_dp, 1, width), F32),
        dma((2, chips)),
        dma((2, chips)),
        dma((2, chips)),
        dma((2, chips)),
        dma((2, n_blk)),
        dma((2, n_dp)),
        *sz.item_scratch(width),
        *sz.item_scratch(hq),
        *sz.item_scratch(2 * HS),
    ]
    smem = pl.BlockSpec(memory_space=pltpu.SMEM)
    vmem = pl.BlockSpec(memory_space=pltpu.VMEM)
    shape = jax.ShapeDtypeStruct
    d_in, g_query, g_key, g_value, g_out, g_gain = pl.pallas_call(
        functools.partial(kernel, sz),
        out_shape=(
            shape((tok, width), BF16),
            shape((sz.rows, hq), F32),
            shape((sz.rows, HS), F32),
            shape((sz.rows, HS), F32),
            shape((sz.rows, width), F32),
            shape((1, sz.rows), F32),
        ),
        in_specs=[smem, smem] + [vmem] * 7,
        out_specs=(vmem,) * 6,
        scratch_shapes=scratch,
        compiler_params=pltpu.CompilerParams(
            collective_id=0, has_side_effects=True, vmem_limit_bytes=60 * 1024 * 1024
        ),
    )(prefix_len, bound, inputs[0], upstream[0], gain[None], w_query, w_key, w_value, w_out)
    return d_in[None], g_query, g_key, g_value, g_out, g_gain[0]


def solution(mesh):
    placed = (P("dp", "blk", None), P("dp", "blk", None), P(), P(), P(), P(), P(), P("dp"), P("dp"))
    return jax.shard_map(
        functools.partial(per_device, mesh.shape["dp"], mesh.shape["blk"]),
        mesh=mesh,
        in_specs=placed,
        out_specs=(
            P("dp", "blk", None),
            P("blk", None),
            P("blk", None),
            P("blk", None),
            P("blk", None),
            P("blk"),
        ),
        check_vma=False,
    )
```
